256 devices in a mesh: seq: 16 (over z_lo, y), ch: 8 (over x, core), batch: 2 (over z_hi).
Axes of the slice: x: 4, y: 4, z: 8 (z_hi: 2, z_lo: 4; z = z_hi * 4 + z_lo), core: 2. Of those that a mesh axis runs over, the one named last changes fastest.
Arguments:
- query_gate: bfloat16 [2, 16384, 2048], P('batch', ('seq', 'ch')), may hold values from -6 to 6
- key_gate: bfloat16 [2, 16384, 2048], P('batch', ('seq', 'ch')), may hold values from -6 to 6
- value_input: bfloat16 [2, 16384, 2048], P('batch', ('seq', 'ch')), may hold values from -6 to 6
- long_filter: bfloat16 [16384, 2048], P('seq', 'ch'), may hold values from -0.046875 to 0.046875
- skip_gain: float32 [2048], replicated, may hold values from -4 to 4
Outputs:
- gated: bfloat16 [2, 16384, 2048], P('batch', ('seq', 'ch'))
The draws below stay inside these ranges and needn't reach their ends.
All inputs are finite; a program needn't handle non-finite values.
Results may differ from the reference program's by a relative error of at most 0.0053.
Values may be sent and summed in bfloat16 or wider, within the bound.
No kernel may reach another device: no remote copies, remote signals or barrier semaphores. Data moves between devices by JAX's collectives and lax.ppermute only.
A program may use at most 128 MiB of HBM per device.

```python
import jax
import jax.numpy as jnp
from jax import lax

D = 2048
SEQ_LEN = 16384
SEQS = 2


def level_of(own_key, dims, shards, smallest, largest):
    def one(dim, shards_of):
        steps = jax.random.uniform(jax.random.fold_in(jax.random.fold_in(own_key, 6), dim), (shards_of,), jnp.float32, smallest / len(shards), largest / len(shards))
        return jnp.repeat(jnp.exp(steps), dims[dim] // shards_of).reshape((-1,) + (1,) * (len(dims) - dim - 1))

    loudness = one(*shards[0])
    for cut in shards[1:]:
        loudness = loudness * one(*cut)
    return loudness


def normal_values(own_key, dims, spread, limit, split=(), kind=jnp.bfloat16):
    drawn = spread * jax.random.normal(own_key, dims, jnp.float32)
    if split:
        drawn = drawn * level_of(own_key, dims, split, -0.22, 0.18)
    return jnp.clip(drawn, -limit, limit).astype(kind)


def setup_inputs(seed: int = 0) -> dict:
    arg_keys = jax.random.split(jax.random.key(seed), 6)
    query_gate = normal_values(arg_keys[0], (SEQS, SEQ_LEN, D), 1.0, 6.0, ((0, 2), (1, 128)))
    key_gate = normal_values(arg_keys[1], (SEQS, SEQ_LEN, D), 1.0, 6.0, ((0, 2), (1, 128)))
    value_input = normal_values(arg_keys[2], (SEQS, SEQ_LEN, D), 1.0, 6.0, ((0, 2), (1, 128)))
    long_filter = normal_values(arg_keys[3], (SEQ_LEN, D), SEQ_LEN ** -0.5, 0.046875, ((0, 16), (1, 8)))
    skip_gain = normal_values(arg_keys[4], (D,), 1.0, 4.0, (), jnp.float32)
    return {"query_gate": query_gate, "key_gate": key_gate, "value_input": value_input, "long_filter": long_filter, "skip_gain": skip_gain}


def reference(query_gate, key_gate, value_input, long_filter, skip_gain):
    mixed_in = (key_gate.astype(jnp.float32) * value_input.astype(jnp.float32)).astype(jnp.bfloat16)
    signal = lax.optimization_barrier(mixed_in).astype(jnp.float32)
    kernel = long_filter.astype(jnp.float32)
    seq_len = signal.shape[1]
    channels = signal.shape[2]
    group_size = min(256, channels)
    groups = channels // group_size
    sig_blocks = signal.reshape(signal.shape[0], seq_len, groups, group_size).transpose(2, 0, 1, 3)
    ker_blocks = kernel.reshape(seq_len, groups, group_size).transpose(1, 0, 2)

    def convolve(operands):
        sig_part, ker_part = operands
        spectrum = jnp.fft.rfft(sig_part, n=2 * seq_len, axis=1) * jnp.fft.rfft(ker_part, n=2 * seq_len, axis=0)[None]
        return jnp.fft.irfft(spectrum, n=2 * seq_len, axis=1)[:, :seq_len].astype(sig_part.dtype)

    convolved = lax.map(convolve, (sig_blocks, ker_blocks))
    convolved = convolved.transpose(1, 2, 0, 3).reshape(signal.shape).astype(jnp.bfloat16)
    convolved = lax.optimization_barrier(convolved).astype(jnp.float32)
    joined = convolved + skip_gain[None, None, :] * signal
    return (query_gate.astype(jnp.float32) * joined).astype(jnp.bfloat16)
```

```python
import jax
import jax.numpy as jnp
from jax import lax
from jax.experimental import pallas as pl
from jax.experimental.pallas import tpu as pltpu
from jax.sharding import PartitionSpec as P

F32 = jnp.float32
BF = jnp.bfloat16
ALL = ("batch", "seq", "ch")
VM = pl.BlockSpec(memory_space=pltpu.VMEM)


def mix_kernel(k_ref, v_ref, o_ref):
    for ch in range(8):
        cols = slice(ch * 256, (ch + 1) * 256)
        mixed = (k_ref[:, cols].astype(F32) * v_ref[:, cols].astype(F32)).astype(BF)
        turned = mixed.astype(F32).T.reshape(16, 2, 8, 128).astype(BF)
        for b in range(2):
            o_ref[b, :, ch] = turned[:, b]


def filter_kernel(b_ref, f_ref, o_ref):
    turned = f_ref[...].astype(F32).T.reshape(16, 2, 8, 1024)
    o_ref[...] = jnp.where(b_ref[0] == 0, turned[:, 0], turned[:, 1]).astype(BF)


def gate_kernel(c_ref, q_ref, k_ref, v_ref, s_ref, o_ref):
    for ch in range(8):
        cols = slice(ch * 256, (ch + 1) * 256)
        rows = jnp.stack([c_ref[b, :, ch].astype(F32) for b in range(2)], axis=1)
        conv = rows.reshape(256, 128).T
        mixed = (k_ref[:, cols].astype(F32) * v_ref[:, cols].astype(F32)).astype(BF)
        joined = conv + s_ref[:, cols] * mixed.astype(F32)
        o_ref[:, cols] = (q_ref[:, cols].astype(F32) * joined).astype(BF)


def conv_kernel(x_ref, f_ref, o_ref, xf, hf, xs, tt, acc):
    PAD=256
    ROWS=1024
    for b in range(2):
        xf[b, 0:PAD, :] = jnp.zeros((PAD,128),F32)
        xf[b, PAD:, :] = x_ref[b*128:(b+1)*128].astype(F32).reshape(ROWS,128)
    fv = f_ref[...].astype(F32).reshape(128,1024)
    for q in range(8): hf[q] = fv[:, q*128:(q+1)*128]
    row_i = lax.broadcasted_iota(jnp.int32,(128,128),0)
    col_i = lax.broadcasted_iota(jnp.int32,(128,128),1)
    keep = col_i >= row_i

    def skew(c, m_s, q):
        row = hf[q, pl.ds(m_s*8 + c, 1), :]
        return pltpu.roll(jnp.broadcast_to(row,(128,128)), 0, 1, stride=1, stride_axis=0)

    def channel(c, _):
        for e0 in range(16):
            for b in range(2):
                for h in range(2):
                    v = xf[b, pl.ds(PAD + (h - 2*e0)*8 + c, 64, stride=16), :]
                    xs[b*64:(b+1)*64, e0*256+h*128:e0*256+(h+1)*128] = v.astype(BF)
        def build(s, carry):
            prev, gprev = carry
            for q in range(0,8,2):
                r0 = skew(c, s, q)
                g0 = jnp.where(keep, r0, prev).astype(BF)
                r1 = skew(c, s, q+1)
                g1 = jnp.where(keep, r1, r0).astype(BF)
                base = pl.multiple_of(s*1024 + q*128, 256)
                tt[pl.ds(base,128), 0:128] = g0
                tt[pl.ds(base+128,128), 128:256] = g0
                tt[pl.ds(base,128), 128:256] = g1
                tt[pl.ds(base+128,128), 0:128] = gprev
                prev, gprev = r1, g1
            return prev, gprev
        lax.fori_loop(0,16,build,(jnp.zeros((128,128),F32),jnp.zeros((128,128),BF)))
        for e1 in range(4):
            n = 64-16*e1
            lhs = xs[...].reshape(2,64,4096)[:, :n, :].reshape(2*n,4096)
            p = jnp.dot(lhs, tt[e1*4096:(e1+1)*4096,:], preferred_element_type=F32).reshape(2,n,256)
            if e1==0: acc[...] = p
            else: acc[:,16*e1:,:] += p
        for b in range(2):
            for h in range(2):
                xf[b, pl.ds(PAD + h*8 + c, 64, stride=16), :] = acc[b, :, h*128:(h+1)*128]
        return 0
    lax.fori_loop(0,8,channel,0)
    for b in range(2):
        o_ref[b*128:(b+1)*128] = xf[b, PAD:, :].reshape(128,8,128).astype(BF)


def conv(x, f):
    return pl.pallas_call(
        conv_kernel,
        out_shape=jax.ShapeDtypeStruct((256, 8, 128), BF),
        in_specs=[VM, VM],
        out_specs=VM,
        scratch_shapes=[
            pltpu.VMEM((2, 1280, 128), F32),
            pltpu.VMEM((8, 128, 128), F32),
            pltpu.VMEM((128, 4096), BF),
            pltpu.VMEM((16384, 256), BF),
            pltpu.VMEM((2, 64, 256), F32),
        ],
        compiler_params=pltpu.CompilerParams(vmem_limit_bytes=40 * 2**20),
    )(x, f)


def body(query_gate, key_gate, value_input, long_filter, skip_gain):
    q, k, v = query_gate[0], key_gate[0], value_input[0]
    params = pltpu.CompilerParams(vmem_limit_bytes=40 * 2**20)
    own = lax.axis_index("batch").astype(jnp.int32).reshape(1)
    taps = pl.pallas_call(
        filter_kernel,
        out_shape=jax.ShapeDtypeStruct((16, 8, 1024), BF),
        in_specs=[pl.BlockSpec(memory_space=pltpu.SMEM), VM],
        out_specs=VM,
        compiler_params=params,
    )(own, long_filter)
    taps = lax.all_to_all(taps, "seq", split_axis=0, concat_axis=0, tiled=True)
    mixed = pl.pallas_call(
        mix_kernel,
        out_shape=jax.ShapeDtypeStruct((2, 16, 8, 8, 128), BF),
        in_specs=[VM, VM],
        out_specs=VM,
        compiler_params=params,
    )(k, v).reshape(256, 8, 128)
    mixed = lax.all_to_all(mixed, ALL, split_axis=0, concat_axis=0, tiled=True)
    conv_out = conv(mixed, taps)
    back = lax.all_to_all(conv_out, ALL, split_axis=0, concat_axis=0, tiled=True)
    return pl.pallas_call(
        gate_kernel,
        out_shape=jax.ShapeDtypeStruct((128, 2048), BF),
        in_specs=[VM] * 5,
        out_specs=VM,
        compiler_params=params,
    )(back.reshape(2, 16, 8, 8, 128), q, k, v, skip_gain.reshape(1, 2048))[None]


def solution(mesh):
    return jax.shard_map(
        body,
        mesh=mesh,
        in_specs=(
            P("batch", ("seq", "ch"), None),
            P("batch", ("seq", "ch"), None),
            P("batch", ("seq", "ch"), None),
            P("seq", "ch"),
            P(),
        ),
        out_specs=P("batch", ("seq", "ch"), None),
        check_vma=False,
    )
```

```python
import jax
import jax.numpy as jnp
from jax import lax
from jax.experimental import pallas as pl
from jax.experimental.pallas import tpu as pltpu
from jax.sharding import PartitionSpec as P

F32 = jnp.float32
BF = jnp.bfloat16
ALL = ("batch", "seq", "ch")
VM = pl.BlockSpec(memory_space=pltpu.VMEM)


def mix_kernel(k_ref, v_ref, o_ref):
    for ch in range(8):
        cols = slice(ch * 256, (ch + 1) * 256)
        mixed = (k_ref[:, cols].astype(F32) * v_ref[:, cols].astype(F32)).astype(BF)
        turned = mixed.astype(F32).T.reshape(16, 2, 8, 128).astype(BF)
        for b in range(2):
            o_ref[b, :, ch] = turned[:, b]


def filter_kernel(b_ref, f_ref, o_ref):
    turned = f_ref[...].astype(F32).T.reshape(16, 2, 8, 1024)
    o_ref[...] = jnp.where(b_ref[0] == 0, turned[:, 0], turned[:, 1]).astype(BF)


def gate_kernel(c_ref, q_ref, k_ref, v_ref, s_ref, o_ref):
    for ch in range(8):
        cols = slice(ch * 256, (ch + 1) * 256)
        rows = jnp.stack([c_ref[b, :, ch].astype(F32) for b in range(2)], axis=1)
        conv = rows.reshape(256, 128).T
        mixed = (k_ref[:, cols].astype(F32) * v_ref[:, cols].astype(F32)).astype(BF)
        joined = conv + s_ref[:, cols] * mixed.astype(F32)
        o_ref[:, cols] = (q_ref[:, cols].astype(F32) * joined).astype(BF)


def conv_kernel(x_ref, f_ref, o_ref, xf, hf, xa, xb, yf):
    PAD=256
    ROWS=1024
    for b in range(2):
        xf[b, 0:PAD, :] = jnp.zeros((PAD,128),F32)
        xf[b, PAD:, :] = x_ref[b*128:(b+1)*128].astype(F32).reshape(ROWS,128)
    fv = f_ref[...].astype(F32).reshape(128,1024)
    for q in range(8): hf[q] = fv[:, q*128:(q+1)*128]
    row_i = lax.broadcasted_iota(jnp.int32,(128,128),0)
    col_i = lax.broadcasted_iota(jnp.int32,(128,128),1)
    keep = col_i >= row_i

    def skew(c, m):
        row = hf[m%8, pl.ds((m//8)*8 + c, 1), :]
        return pltpu.roll(jnp.broadcast_to(row,(128,128)), 0, 1, stride=1, stride_axis=0)

    def shifted(c, xs, e0):
        for b in range(2):
            for h in range(2):
                v = xf[b, pl.ds(PAD + (h - 2*e0)*8 + c, 64, stride=16), :]
                xs[b*64:(b+1)*64, e0*256+h*128:e0*256+(h+1)*128] = v.astype(BF)

    def channel(c, xs, nxt):
        prev = jnp.zeros((128,128),F32); gprev=jnp.zeros((128,128),BF)
        total=None
        for e1 in range(4):
            n = 64-16*e1
            lhs = xs[...].reshape(2,64,4096)[:, :n, :].reshape(2*n,4096)
            p=None
            for e0 in range(16):
                e=16*e1+e0
                r0=skew(c,2*e); g0=jnp.where(keep,r0,prev).astype(BF)
                r1=skew(c,2*e+1); g1=jnp.where(keep,r1,r0).astype(BF)
                rhs = jnp.concatenate([jnp.concatenate([g0,g1],axis=1), jnp.concatenate([gprev,g0],axis=1)],axis=0)
                prev=r1; gprev=g1
                pp = jnp.dot(lhs[:, e0*256:(e0+1)*256], rhs, preferred_element_type=F32)
                p = pp if p is None else p+pp
                if nxt is not None and e0%4==3:
                    shifted(c+1, nxt, e//4)
            p=p.reshape(2,n,256)
            for b in range(2):
                for h in range(2):
                    at=pl.ds((32*e1*8 + h*8) + c, n, stride=16)
                    val=p[b,:,h*128:(h+1)*128]
                    if e1==0: yf[b, at, :] = val
                    else: yf[b, at, :] = yf[b, at, :] + val
    for e0 in range(16): shifted(0, xa, e0)
    def pair(i, _):
        channel(2*i, xa, xb)
        channel(2*i+1, xb, xa)
        return 0
    lax.fori_loop(0,3,pair,0)
    channel(6, xa, xb)
    channel(7, xb, None)
    for b in range(2):
        o_ref[b*128:(b+1)*128] = yf[b].reshape(128,8,128).astype(BF)


def conv(x, f):
    return pl.pallas_call(
        conv_kernel,
        out_shape=jax.ShapeDtypeStruct((256, 8, 128), BF),
        in_specs=[VM, VM],
        out_specs=VM,
        scratch_shapes=[
            pltpu.VMEM((2, 1280, 128), F32),
            pltpu.VMEM((8, 128, 128), F32),
            pltpu.VMEM((128, 4096), BF),
            pltpu.VMEM((128, 4096), BF),
            pltpu.VMEM((2, 1024, 128), F32),
        ],
        compiler_params=pltpu.CompilerParams(vmem_limit_bytes=40 * 2**20),
    )(x, f)


def body(query_gate, key_gate, value_input, long_filter, skip_gain):
    q, k, v = query_gate[0], key_gate[0], value_input[0]
    params = pltpu.CompilerParams(vmem_limit_bytes=40 * 2**20)
    own = lax.axis_index("batch").astype(jnp.int32).reshape(1)
    taps = pl.pallas_call(
        filter_kernel,
        out_shape=jax.ShapeDtypeStruct((16, 8, 1024), BF),
        in_specs=[pl.BlockSpec(memory_space=pltpu.SMEM), VM],
        out_specs=VM,
        compiler_params=params,
    )(own, long_filter)
    taps = lax.all_to_all(taps, "seq", split_axis=0, concat_axis=0, tiled=True)
    mixed = pl.pallas_call(
        mix_kernel,
        out_shape=jax.ShapeDtypeStruct((2, 16, 8, 8, 128), BF),
        in_specs=[VM, VM],
        out_specs=VM,
        compiler_params=params,
    )(k, v).reshape(256, 8, 128)
    mixed = lax.all_to_all(mixed, ALL, split_axis=0, concat_axis=0, tiled=True)
    conv_out = conv(mixed, taps)
    back = lax.all_to_all(conv_out, ALL, split_axis=0, concat_axis=0, tiled=True)
    return pl.pallas_call(
        gate_kernel,
        out_shape=jax.ShapeDtypeStruct((128, 2048), BF),
        in_specs=[VM] * 5,
        out_specs=VM,
        compiler_params=params,
    )(back.reshape(2, 16, 8, 8, 128), q, k, v, skip_gain.reshape(1, 2048))[None]


def solution(mesh):
    return jax.shard_map(
        body,
        mesh=mesh,
        in_specs=(
            P("batch", ("seq", "ch"), None),
            P("batch", ("seq", "ch"), None),
            P("batch", ("seq", "ch"), None),
            P("seq", "ch"),
            P(),
        ),
        out_specs=P("batch", ("seq", "ch"), None),
        check_vma=False,
    )
```

```python
import jax
import jax.numpy as jnp
from jax import lax
from jax.experimental import pallas as pl
from jax.experimental.pallas import tpu as pltpu
from jax.sharding import PartitionSpec as P

F32 = jnp.float32
BF = jnp.bfloat16
ALL = ("batch", "seq", "ch")
VM = pl.BlockSpec(memory_space=pltpu.VMEM)
ANY = pl.BlockSpec(memory_space=pl.ANY)


def start_kernel(f_ref, k_ref, v_ref, o0, o1, o2, o3, m_ref, fb, kb, vb, mb, sems):
    loads = [
        pltpu.make_async_copy(src, dst, sems.at[i])
        for i, (src, dst) in enumerate(((k_ref, kb), (v_ref, vb), (f_ref, fb)))
    ]
    for load in loads:
        load.start()
    loads[0].wait()
    loads[1].wait()
    for ch in range(8):
        cols = slice(ch * 256, (ch + 1) * 256)
        mixed = (kb[:, cols].astype(F32) * vb[:, cols].astype(F32)).astype(BF)
        turned = mixed.astype(F32).T.reshape(16, 2, 8, 128).astype(BF)
        for b in range(2):
            mb[b, :, ch] = turned[:, b]
    store = pltpu.make_async_copy(mb, m_ref, sems.at[3])
    store.start()
    loads[2].wait()
    turned = fb[...].astype(F32).T.reshape(16, 2, 8, 1024)
    own = jnp.where(lax.axis_index("batch") == 0, turned[:, 0], turned[:, 1]).astype(BF).reshape(4, 4, 8, 1024)
    for z in range(4):

        @pl.when(lax.axis_index("seq") // 4 == z)
        def _():
            for q, o_ref in enumerate((o0, o1, o2, o3)):
                o_ref[...] = own[z ^ q]

    store.wait()


def turn_kernel(*refs):
    for r in range(4):
        for q in range(4):
            refs[4 + r][q] = refs[q][(lax.axis_index("seq") % 4) ^ r]


def gate_kernel(c_ref, q_ref, k_ref, v_ref, s_ref, o_ref):
    for ch in range(8):
        cols = slice(ch * 256, (ch + 1) * 256)
        rows = jnp.stack([c_ref[b, :, ch].astype(F32) for b in range(2)], axis=1)
        conv = rows.reshape(256, 128).T
        mixed = (k_ref[:, cols].astype(F32) * v_ref[:, cols].astype(F32)).astype(BF)
        joined = conv + s_ref[:, cols] * mixed.astype(F32)
        o_ref[:, cols] = (q_ref[:, cols].astype(F32) * joined).astype(BF)


def read_taps(hf, f_refs):
    seq = lax.axis_index("seq")
    for y, f_ref in enumerate(f_refs):
        for z in range(4):
            block = ((seq // 4) ^ z) * 4 + ((seq % 4) ^ y)
            rows = pl.ds(pl.multiple_of(block * 8, 8), 8)
            fv = f_ref[z].astype(F32)
            for q in range(8):
                hf[q, rows, :] = fv[:, q * 128 : (q + 1) * 128]


def upper():
    shape = (128, 128)
    return lax.broadcasted_iota(jnp.int32, shape, 1) >= lax.broadcasted_iota(jnp.int32, shape, 0)


def skew(hf, c, m):
    row = hf[m % 8, pl.ds((m // 8) * 8 + c, 1), :]
    turned = pltpu.roll(jnp.broadcast_to(row, (128, 128)), 0, 1, stride=1, stride_axis=0)
    return turned.astype(BF)


def conv_kernel(x_ref, f0_ref, f1_ref, f2_ref, f3_ref, o_ref, xf, hf, xa, xb, yf):
    pad = 256
    for b in range(2):
        xf[b, 0:pad, :] = jnp.zeros((pad, 128), F32)
        xf[b, pad:, :] = x_ref[b * 128 : (b + 1) * 128].astype(F32).reshape(1024, 128)
    read_taps(hf, (f0_ref, f1_ref, f2_ref, f3_ref))
    keep = upper()

    def shifted(c, xs, e0):
        for b in range(2):
            for h in range(2):
                v = xf[b, pl.ds(pad + (h - 2 * e0) * 8 + c, 64, stride=16), :]
                xs[b * 64 : (b + 1) * 64, e0 * 256 + h * 128 : e0 * 256 + (h + 1) * 128] = v.astype(BF)

    def channel(c, xs, after, nxt):
        prev = jnp.zeros((128, 128), BF)
        gprev = jnp.zeros((128, 128), BF)
        for e1 in range(4):
            n = 64 - 16 * e1
            lhs = xs[...].reshape(2, 64, 4096)[:, :n, :].reshape(2 * n, 4096)
            total = None
            for e0 in range(16):
                e = 16 * e1 + e0
                r0 = skew(hf, c, 2 * e)
                g0 = jnp.where(keep, r0, prev)
                r1 = skew(hf, c, 2 * e + 1)
                g1 = jnp.where(keep, r1, r0)
                top = jnp.concatenate([g0, g1], axis=1)
                low = jnp.concatenate([gprev, g0], axis=1)
                prev, gprev = r1, g1
                rhs = jnp.concatenate([top, low], axis=0)
                part = jnp.dot(lhs[:, e0 * 256 : (e0 + 1) * 256], rhs, preferred_element_type=F32)
                total = part if total is None else total + part
                if e0 % 4 == 3:
                    shifted(after, nxt, e // 4)
            total = total.reshape(2, n, 256)
            for b in range(2):
                for h in range(2):
                    at = pl.ds(32 * e1 * 8 + h * 8 + c, n, stride=16)
                    part = total[b, :, h * 128 : (h + 1) * 128]
                    yf[b, at, :] = part if e1 == 0 else yf[b, at, :] + part

    for e0 in range(16):
        shifted(0, xa, e0)

    def pair(i, _):
        channel(2 * i, xa, 2 * i + 1, xb)
        channel(2 * i + 1, xb, jnp.minimum(2 * i + 2, 7), xa)
        return 0

    lax.fori_loop(0, 4, pair, 0)
    for b in range(2):
        o_ref[b * 128 : (b + 1) * 128] = yf[b].reshape(128, 8, 128).astype(BF)


def conv(x, fs):
    return pl.pallas_call(
        conv_kernel,
        out_shape=jax.ShapeDtypeStruct((256, 8, 128), BF),
        in_specs=[VM] * 5,
        out_specs=VM,
        scratch_shapes=[
            pltpu.VMEM((2, 1280, 128), F32),
            pltpu.VMEM((8, 128, 128), F32),
            pltpu.VMEM((128, 4096), BF),
            pltpu.VMEM((128, 4096), BF),
            pltpu.VMEM((2, 1024, 128), F32),
        ],
        compiler_params=pltpu.CompilerParams(vmem_limit_bytes=32 * 2**20),
    )(x, *fs)


def swap(parts, step):
    return [parts[0]] + [
        lax.ppermute(parts[r], "seq", [(i, i ^ (r * step)) for i in range(16)])
        for r in range(1, 4)
    ]


def body(query_gate, key_gate, value_input, long_filter, skip_gain):
    q, k, v = query_gate[0], key_gate[0], value_input[0]
    params = pltpu.CompilerParams(vmem_limit_bytes=40 * 2**20)
    quarter = jax.ShapeDtypeStruct((4, 8, 1024), BF)
    *parts, mixed = pl.pallas_call(
        start_kernel,
        out_shape=[quarter] * 4 + [jax.ShapeDtypeStruct((2, 16, 8, 8, 128), BF)],
        in_specs=[ANY] * 3,
        out_specs=[VM] * 4 + [ANY],
        scratch_shapes=[
            pltpu.VMEM((1024, 256), BF),
            pltpu.VMEM((128, 2048), BF),
            pltpu.VMEM((128, 2048), BF),
            pltpu.VMEM((2, 16, 8, 8, 128), BF),
            pltpu.SemaphoreType.DMA((4,)),
        ],
        compiler_params=pltpu.CompilerParams(vmem_limit_bytes=60 * 2**20),
    )(long_filter, k, v)
    parts = swap(parts, 4)
    parts = pl.pallas_call(
        turn_kernel,
        out_shape=[quarter] * 4,
        in_specs=[VM] * 4,
        out_specs=[VM] * 4,
        compiler_params=params,
        cost_estimate=pl.CostEstimate(flops=2 * 10**10, bytes_accessed=0, transcendentals=0),
    )(*parts)
    parts = swap(parts, 1)
    mixed = lax.all_to_all(mixed.reshape(256, 8, 128), ALL, split_axis=0, concat_axis=0, tiled=True)
    conv_out = conv(mixed, parts)
    back = lax.all_to_all(conv_out, ALL, split_axis=0, concat_axis=0, tiled=True)
    return pl.pallas_call(
        gate_kernel,
        out_shape=jax.ShapeDtypeStruct((128, 2048), BF),
        in_specs=[VM] * 5,
        out_specs=VM,
        compiler_params=params,
    )(back.reshape(2, 16, 8, 8, 128), q, k, v, skip_gain.reshape(1, 2048))[None]


def solution(mesh):
    return jax.shard_map(
        body,
        mesh=mesh,
        in_specs=(
            P("batch", ("seq", "ch"), None),
            P("batch", ("seq", "ch"), None),
            P("batch", ("seq", "ch"), None),
            P("seq", "ch"),
            P(),
        ),
        out_specs=P("batch", ("seq", "ch"), None),
        check_vma=False,
    )
```

```python
import jax
import jax.numpy as jnp
from jax import lax
from jax.experimental import pallas as pl
from jax.experimental.pallas import tpu as pltpu
from jax.sharding import PartitionSpec as P

F32 = jnp.float32
BF = jnp.bfloat16
HOPS = (0, 1, -1, 2)
ALL = ("batch", "seq", "ch")
VM = pl.BlockSpec(memory_space=pltpu.VMEM)
ANY = pl.BlockSpec(memory_space=pl.ANY)


def start_kernel(f_ref, k_ref, v_ref, o0, o1, o2, o3, m_ref, fb, kb, vb, mb, ob, sems):
    loads = []
    for part in range(2):
        cols = pl.ds(part * 1024, 1024)
        for src, dst in ((k_ref, kb), (v_ref, vb)):
            loads.append(pltpu.make_async_copy(src.at[:, cols], dst.at[:, cols], sems.at[len(loads)]))
    loads.append(pltpu.make_async_copy(f_ref, fb, sems.at[4]))
    for load in loads:
        load.start()
    stores = []
    for part in range(2):
        loads[2 * part].wait()
        loads[2 * part + 1].wait()
        for ch in range(4 * part, 4 * part + 4):
            cols = slice(ch * 256, (ch + 1) * 256)
            mixed = (kb[:, cols].astype(F32) * vb[:, cols].astype(F32)).astype(BF)
            turned = mixed.astype(F32).T.reshape(16, 2, 8, 128).astype(BF)
            for b in range(2):
                mb[b, :, ch] = turned[:, b]
        at = (slice(None), slice(None), pl.ds(4 * part, 4))
        stores.append(pltpu.make_async_copy(mb.at[at], m_ref.at[at], sems.at[5 + part]))
        stores[-1].start()
    loads[4].wait()
    turned = fb[...].astype(F32).T.reshape(16, 2, 8, 1024).astype(BF)
    for b in range(2):
        ob[b] = turned[:, b]
    ring = lax.axis_index("batch") * 4 + lax.axis_index("seq") // 4
    for o_ref, hop in zip((o0, o1, o2, o3), HOPS):
        to = (ring + (hop + 8)) % 8
        o_ref[...] = ob[to // 4, pl.ds((to % 4) * 4, 4)]
    for store in stores:
        store.wait()


def turn_kernel(*refs):
    for r in range(4):
        for q in range(4):
            refs[4 + r][q] = refs[q][(lax.axis_index("seq") % 4) ^ r]


def gate_kernel(c_ref, q_ref, k_ref, v_ref, s_ref, o_ref):
    for ch in range(8):
        cols = slice(ch * 256, (ch + 1) * 256)
        rows = jnp.stack([c_ref[b, :, ch].astype(F32) for b in range(2)], axis=1)
        conv = rows.reshape(256, 128).T
        mixed = (k_ref[:, cols].astype(F32) * v_ref[:, cols].astype(F32)).astype(BF)
        joined = conv + s_ref[:, cols] * mixed.astype(F32)
        o_ref[:, cols] = (q_ref[:, cols].astype(F32) * joined).astype(BF)


def read_taps(hf, f_refs):
    seq = lax.axis_index("seq")
    for y, f_ref in enumerate(f_refs):
        for z, hop in enumerate(HOPS):
            block = ((seq // 4 + (8 - hop)) % 4) * 4 + ((seq % 4) ^ y)
            rows = pl.ds(pl.multiple_of(block * 8, 8), 8)
            fv = f_ref[z].astype(F32)
            for q in range(8):
                hf[q, rows, :] = fv[:, q * 128 : (q + 1) * 128]


def upper():
    shape = (128, 128)
    return lax.broadcasted_iota(jnp.int32, shape, 1) >= lax.broadcasted_iota(jnp.int32, shape, 0)


def skew(hf, c, m):
    row = hf[m % 8, pl.ds((m // 8) * 8 + c, 1), :]
    turned = pltpu.roll(jnp.broadcast_to(row, (128, 128)), 0, 1, stride=1, stride_axis=0)
    return turned.astype(BF)


def conv_kernel(x_ref, f0_ref, f1_ref, f2_ref, f3_ref, o_ref, xf, hf, xa, xb, xg, yg, yf):
    for b in range(2):
        xf[b] = x_ref[b * 128 : (b + 1) * 128].astype(F32).reshape(1024, 128)
        for h in range(2):
            xg[b, h, 0:16, :] = jnp.zeros((16, 128), F32)
    read_taps(hf, (f0_ref, f1_ref, f2_ref, f3_ref))
    keep = upper()

    def pull(c):
        for b in range(2):
            for h in range(2):
                xg[b, h, 16:80, :] = xf[b, pl.ds(h * 8 + c, 64, stride=16), :]

    def shifted(xs, e0):
        for b in range(2):
            for h in range(2):
                cols = slice(e0 * 256 + h * 128, e0 * 256 + (h + 1) * 128)
                xs[b * 64 : (b + 1) * 64, cols] = xg[b, h, 16 - e0 : 80 - e0, :].astype(BF)

    def channel(c, xs, nxt):
        prev = jnp.zeros((128, 128), BF)
        gprev = jnp.zeros((128, 128), BF)
        for e1 in range(4):
            n = 64 - 16 * e1
            lhs = xs[...].reshape(2, 64, 4096)[:, :n, :].reshape(2 * n, 4096)
            total = None
            for e0 in range(16):
                e = 16 * e1 + e0
                r0 = skew(hf, c, 2 * e)
                g0 = jnp.where(keep, r0, prev)
                r1 = skew(hf, c, 2 * e + 1)
                g1 = jnp.where(keep, r1, r0)
                top = jnp.concatenate([g0, g1], axis=1)
                low = jnp.concatenate([gprev, g0], axis=1)
                prev, gprev = r1, g1
                rhs = jnp.concatenate([top, low], axis=0)
                part = jnp.dot(lhs[:, e0 * 256 : (e0 + 1) * 256], rhs, preferred_element_type=F32)
                total = part if total is None else total + part
                if e == 1 and c < 7:
                    pull(c + 1)
                if e0 % 4 == 3 and c < 7:
                    shifted(nxt, e // 4)
            total = total.reshape(2, n, 256)
            for b in range(2):
                for h in range(2):
                    part = total[b, :, h * 128 : (h + 1) * 128]
                    if e1 == 0:
                        yg[b, h] = part
                    elif e1 < 3:
                        yg[b, h, 16 * e1 :, :] += part
                    else:
                        yf[b, pl.ds(h * 8 + c, 48, stride=16), :] = yg[b, h, :48, :]
                        yf[b, pl.ds(768 + h * 8 + c, 16, stride=16), :] = yg[b, h, 48:, :] + part

    pull(0)
    for e0 in range(16):
        shifted(xa, e0)

    for c in range(8):
        channel(c, (xa, xb)[c % 2], (xb, xa)[c % 2])
    for b in range(2):
        o_ref[b * 128 : (b + 1) * 128] = yf[b].reshape(128, 8, 128).astype(BF)


def conv(x, fs):
    return pl.pallas_call(
        conv_kernel,
        out_shape=jax.ShapeDtypeStruct((256, 8, 128), BF),
        in_specs=[VM] * 5,
        out_specs=VM,
        scratch_shapes=[
            pltpu.VMEM((2, 1024, 128), F32),
            pltpu.VMEM((8, 128, 128), F32),
            pltpu.VMEM((128, 4096), BF),
            pltpu.VMEM((128, 4096), BF),
            pltpu.VMEM((2, 2, 80, 128), F32),
            pltpu.VMEM((2, 2, 64, 128), F32),
            pltpu.VMEM((2, 1024, 128), F32),
        ],
        compiler_params=pltpu.CompilerParams(vmem_limit_bytes=32 * 2**20),
    )(x, *fs)


def along_z(parts):
    def at(p, y):
        return (p % 4 * 4 + y) * 2 + p % 8 // 4

    return [parts[0]] + [
        lax.ppermute(part, ("seq", "batch"), [(at(p, y), at(p + hop, y)) for p in range(8) for y in range(4)])
        for part, hop in zip(parts[1:], HOPS[1:])
    ]


def along_y(parts):
    return [parts[0]] + [
        lax.ppermute(parts[r], "seq", [(i, i ^ r) for i in range(16)]) for r in range(1, 4)
    ]


def body(query_gate, key_gate, value_input, long_filter, skip_gain):
    q, k, v = query_gate[0], key_gate[0], value_input[0]
    params = pltpu.CompilerParams(vmem_limit_bytes=40 * 2**20)
    quarter = jax.ShapeDtypeStruct((4, 8, 1024), BF)
    *parts, mixed = pl.pallas_call(
        start_kernel,
        out_shape=[quarter] * 4 + [jax.ShapeDtypeStruct((2, 16, 8, 8, 128), BF)],
        in_specs=[ANY] * 3,
        out_specs=[VM] * 4 + [ANY],
        scratch_shapes=[
            pltpu.VMEM((1024, 256), BF),
            pltpu.VMEM((128, 2048), BF),
            pltpu.VMEM((128, 2048), BF),
            pltpu.VMEM((2, 16, 8, 8, 128), BF),
            pltpu.VMEM((2, 16, 8, 1024), BF),
            pltpu.SemaphoreType.DMA((7,)),
        ],
        compiler_params=pltpu.CompilerParams(vmem_limit_bytes=60 * 2**20),
    )(long_filter, k, v)
    parts = along_z(parts)
    parts = pl.pallas_call(
        turn_kernel,
        out_shape=[quarter] * 4,
        in_specs=[VM] * 4,
        out_specs=[VM] * 4,
        compiler_params=params,
        cost_estimate=pl.CostEstimate(flops=2 * 10**10, bytes_accessed=0, transcendentals=0),
    )(*parts)
    parts = along_y(parts)
    mixed = lax.all_to_all(mixed.reshape(256, 8, 128), ALL, split_axis=0, concat_axis=0, tiled=True)
    conv_out = conv(mixed, parts)
    back = lax.all_to_all(conv_out, ALL, split_axis=0, concat_axis=0, tiled=True)
    return pl.pallas_call(
        gate_kernel,
        out_shape=jax.ShapeDtypeStruct((128, 2048), BF),
        in_specs=[VM] * 5,
        out_specs=VM,
        compiler_params=params,
    )(back.reshape(2, 16, 8, 8, 128), q, k, v, skip_gain.reshape(1, 2048))[None]


def solution(mesh):
    return jax.shard_map(
        body,
        mesh=mesh,
        in_specs=(
            P("batch", ("seq", "ch"), None),
            P("batch", ("seq", "ch"), None),
            P("batch", ("seq", "ch"), None),
            P("seq", "ch"),
            P(),
        ),
        out_specs=P("batch", ("seq", "ch"), None),
        check_vma=False,
    )
```

```python
import jax
import jax.numpy as jnp
from jax import lax
from jax.experimental import pallas as pl
from jax.experimental.pallas import tpu as pltpu
from jax.sharding import PartitionSpec as P

F32 = jnp.float32
BF = jnp.bfloat16
HOPS = (0, 1, -1, -2)
ALL = ("batch", "seq", "ch")
VM = pl.BlockSpec(memory_space=pltpu.VMEM)
ANY = pl.BlockSpec(memory_space=pl.ANY)


def start_kernel(f_ref, k_ref, v_ref, o0, o1, o2, o3, m_ref, fb, kb, vb, mb, ob, sems):
    loads = [pltpu.make_async_copy(f_ref, fb, sems.at[0])]
    for part in range(2):
        cols = pl.ds(part * 1024, 1024)
        for src, dst in ((k_ref, kb), (v_ref, vb)):
            loads.append(pltpu.make_async_copy(src.at[:, cols], dst.at[:, cols], sems.at[len(loads)]))
    for load in loads:
        load.start()
    loads[0].wait()
    turned = fb[...].astype(F32).T.reshape(16, 2, 8, 1024).astype(BF)
    for b in range(2):
        ob[b] = turned[:, b]
    ring = lax.axis_index("batch") * 4 + lax.axis_index("seq") // 4
    stores = []
    for o_ref, hop in zip((o0, o1, o2, o3), HOPS):
        to = (ring + (hop + 8)) % 8
        src = ob.at[to // 4, pl.ds((to % 4) * 4, 4)]
        stores.append(pltpu.make_async_copy(src, o_ref, sems.at[5 + len(stores)]))
        stores[-1].start()
    for part in range(2):
        loads[2 * part + 1].wait()
        loads[2 * part + 2].wait()
        for ch in range(4 * part, 4 * part + 4):
            cols = slice(ch * 256, (ch + 1) * 256)
            mixed = (kb[:, cols].astype(F32) * vb[:, cols].astype(F32)).astype(BF)
            turned = mixed.astype(F32).T.reshape(16, 2, 8, 128).astype(BF)
            for b in range(2):
                mb[b, :, ch] = turned[:, b]
        at = (slice(None), slice(None), pl.ds(4 * part, 4))
        stores.append(pltpu.make_async_copy(mb.at[at], m_ref.at[at], sems.at[5 + len(stores)]))
        stores[-1].start()
    for store in stores:
        store.wait()


def turn_kernel(*refs):
    for r in range(4):
        for q in range(4):
            refs[4 + r][q] = refs[q][(lax.axis_index("seq") % 4) ^ r]


def gate_kernel(c_ref, q_ref, k_ref, v_ref, s_ref, o_ref, ob, sems):
    stores = []
    for ch in range(8):
        cols = slice(ch * 256, (ch + 1) * 256)
        rows = jnp.stack([c_ref[b, :, ch].astype(F32) for b in range(2)], axis=1)
        conv = rows.reshape(256, 128).T
        mixed = (k_ref[:, cols].astype(F32) * v_ref[:, cols].astype(F32)).astype(BF)
        joined = conv + s_ref[:, cols] * mixed.astype(F32)
        ob[:, cols] = (q_ref[:, cols].astype(F32) * joined).astype(BF)
        if ch % 2 == 1:
            part = pl.ds((ch - 1) * 256, 512)
            stores.append(pltpu.make_async_copy(ob.at[:, part], o_ref.at[:, part], sems.at[ch // 2]))
            stores[-1].start()
    for store in stores:
        store.wait()


def read_taps(hf, f_refs):
    seq = lax.axis_index("seq")
    for y, f_ref in enumerate(f_refs):
        for z, hop in enumerate(HOPS):
            block = ((seq // 4 + (8 - hop)) % 4) * 4 + ((seq % 4) ^ y)
            rows = pl.ds(pl.multiple_of(block * 8, 8), 8)
            fv = f_ref[z].astype(F32)
            for q in range(8):
                hf[q, rows, :] = fv[:, q * 128 : (q + 1) * 128]


def upper():
    shape = (128, 128)
    return lax.broadcasted_iota(jnp.int32, shape, 1) >= lax.broadcasted_iota(jnp.int32, shape, 0)


def skew(hf, c, m):
    row = hf[m % 8, pl.ds((m // 8) * 8 + c, 1), :]
    turned = pltpu.roll(jnp.broadcast_to(row, (128, 128)), 0, 1, stride=1, stride_axis=0)
    return turned.astype(BF)


def conv_kernel(x_ref, f0_ref, f1_ref, f2_ref, f3_ref, o_ref, xf, hf, xa, xb, xg, yg, yf):
    for b in range(2):
        xf[b] = x_ref[b * 128 : (b + 1) * 128].astype(F32).reshape(1024, 128)
        for h in range(2):
            xg[b, h, 0:16, :] = jnp.zeros((16, 128), F32)
    read_taps(hf, (f0_ref, f1_ref, f2_ref, f3_ref))
    keep = upper()

    def pull(c):
        for b in range(2):
            for h in range(2):
                xg[b, h, 16:80, :] = xf[b, pl.ds(h * 8 + c, 64, stride=16), :]

    def shifted(xs, e0):
        for b in range(2):
            for h in range(2):
                cols = slice(e0 * 256 + h * 128, e0 * 256 + (h + 1) * 128)
                xs[b * 64 : (b + 1) * 64, cols] = xg[b, h, 16 - e0 : 80 - e0, :].astype(BF)

    def channel(c, xs, nxt):
        prev = jnp.zeros((128, 128), BF)
        gprev = jnp.zeros((128, 128), BF)
        for e1 in range(4):
            n = 64 - 16 * e1
            lhs = xs[...].reshape(2, 64, 4096)[:, :n, :].reshape(2 * n, 4096)
            total = None
            for e0 in range(16):
                e = 16 * e1 + e0
                r0 = skew(hf, c, 2 * e)
                g0 = jnp.where(keep, r0, prev)
                r1 = skew(hf, c, 2 * e + 1)
                g1 = jnp.where(keep, r1, r0)
                top = jnp.concatenate([g0, g1], axis=1)
                low = jnp.concatenate([gprev, g0], axis=1)
                prev, gprev = r1, g1
                rhs = jnp.concatenate([top, low], axis=0)
                part = jnp.dot(lhs[:, e0 * 256 : (e0 + 1) * 256], rhs, preferred_element_type=F32)
                total = part if total is None else total + part
                if e == 1 and c < 7:
                    pull(c + 1)
                if e0 % 4 == 3 and c < 7:
                    shifted(nxt, e // 4)
            total = total.reshape(2, n, 256)
            for b in range(2):
                for h in range(2):
                    part = total[b, :, h * 128 : (h + 1) * 128]
                    if e1 == 0:
                        yg[b, h] = part
                    elif e1 < 3:
                        yg[b, h, 16 * e1 :, :] += part
                    else:
                        yf[b, pl.ds(h * 8 + c, 48, stride=16), :] = yg[b, h, :48, :]
                        yf[b, pl.ds(768 + h * 8 + c, 16, stride=16), :] = yg[b, h, 48:, :] + part

    pull(0)
    for e0 in range(16):
        shifted(xa, e0)

    for c in range(8):
        channel(c, (xa, xb)[c % 2], (xb, xa)[c % 2])
    for b in range(2):
        o_ref[b * 128 : (b + 1) * 128] = yf[b].reshape(128, 8, 128).astype(BF)


def conv(x, fs):
    return pl.pallas_call(
        conv_kernel,
        out_shape=jax.ShapeDtypeStruct((256, 8, 128), BF),
        in_specs=[VM] * 5,
        out_specs=VM,
        scratch_shapes=[
            pltpu.VMEM((2, 1024, 128), F32),
            pltpu.VMEM((8, 128, 128), F32),
            pltpu.VMEM((128, 4096), BF),
            pltpu.VMEM((128, 4096), BF),
            pltpu.VMEM((2, 2, 80, 128), F32),
            pltpu.VMEM((2, 2, 64, 128), F32),
            pltpu.VMEM((2, 1024, 128), F32),
        ],
        compiler_params=pltpu.CompilerParams(vmem_limit_bytes=32 * 2**20),
    )(x, *fs)


def along_z(parts):
    def at(p, y):
        return (p % 4 * 4 + y) * 2 + p % 8 // 4

    return [parts[0]] + [
        lax.ppermute(part, ("seq", "batch"), [(at(p, y), at(p + hop, y)) for p in range(8) for y in range(4)])
        for part, hop in zip(parts[1:], HOPS[1:])
    ]


def along_y(parts):
    return [parts[0]] + [
        lax.ppermute(parts[r], "seq", [(i, i ^ r) for i in range(16)]) for r in range(1, 4)
    ]


def body(query_gate, key_gate, value_input, long_filter, skip_gain):
    q, k, v = query_gate[0], key_gate[0], value_input[0]
    params = pltpu.CompilerParams(vmem_limit_bytes=40 * 2**20)
    quarter = jax.ShapeDtypeStruct((4, 8, 1024), BF)
    *parts, mixed = pl.pallas_call(
        start_kernel,
        out_shape=[quarter] * 4 + [jax.ShapeDtypeStruct((2, 16, 8, 8, 128), BF)],
        in_specs=[ANY] * 3,
        out_specs=[ANY] * 5,
        scratch_shapes=[
            pltpu.VMEM((1024, 256), BF),
            pltpu.VMEM((128, 2048), BF),
            pltpu.VMEM((128, 2048), BF),
            pltpu.VMEM((2, 16, 8, 8, 128), BF),
            pltpu.VMEM((2, 16, 8, 1024), BF),
            pltpu.SemaphoreType.DMA((11,)),
        ],
        compiler_params=pltpu.CompilerParams(vmem_limit_bytes=60 * 2**20),
    )(long_filter, k, v)
    parts = along_z(parts)
    parts = pl.pallas_call(
        turn_kernel,
        out_shape=[quarter] * 4,
        in_specs=[VM] * 4,
        out_specs=[VM] * 4,
        compiler_params=params,
        cost_estimate=pl.CostEstimate(flops=2 * 10**10, bytes_accessed=0, transcendentals=0),
    )(*parts)
    parts = along_y(parts)
    mixed = lax.all_to_all(mixed.reshape(256, 8, 128), ALL, split_axis=0, concat_axis=0, tiled=True)
    conv_out = conv(mixed, parts)
    back = lax.all_to_all(conv_out, ALL, split_axis=0, concat_axis=0, tiled=True)
    return pl.pallas_call(
        gate_kernel,
        out_shape=jax.ShapeDtypeStruct((128, 2048), BF),
        in_specs=[VM] * 5,
        out_specs=ANY,
        scratch_shapes=[pltpu.VMEM((128, 2048), BF), pltpu.SemaphoreType.DMA((4,))],
        compiler_params=params,
    )(back.reshape(2, 16, 8, 8, 128), q, k, v, skip_gain.reshape(1, 2048))[None]


def solution(mesh):
    return jax.shard_map(
        body,
        mesh=mesh,
        in_specs=(
            P("batch", ("seq", "ch"), None),
            P("batch", ("seq", "ch"), None),
            P("batch", ("seq", "ch"), None),
            P("seq", "ch"),
            P(),
        ),
        out_specs=P("batch", ("seq", "ch"), None),
        check_vma=False,
    )
```
